32 devices in a mesh: section: 2 (over core), batch: 4 (over y, x), tensor: 4 (over z).
Axes of the slice: x: 2, y: 2, z: 4, core: 2. Of those that a mesh axis runs over, the one named last changes fastest.
Arguments:
- tokens: bfloat16 [16, 1280, 1024], P('batch', 'tensor'), may hold values from -6 to 6
- lengths: int32 [16], P('batch'), may hold values from 30 to 1024, as said below
- ln1_gain: float32 [2, 1280], P('section', 'tensor'), may hold values from 0.5 to 1.5
- ln1_bias: float32 [2, 1280], P('section', 'tensor'), may hold values from -1.5 to 1.5
- w_in: bfloat16 [2, 640, 1280], P('section', 'tensor'), may hold values from -0.15625 to 0.15625
- b_in: float32 [2, 640], P('section', 'tensor'), may hold values from -1.5 to 1.5
- ln2_gain: float32 [2, 640], P('section', 'tensor'), may hold values from 0.5 to 1.5
- ln2_bias: float32 [2, 640], P('section', 'tensor'), may hold values from -1.5 to 1.5
- w_mix: bfloat16 [2, 5, 640, 640], P('section', None, 'tensor'), may hold values from -0.109375 to 0.109375
- b_mix: float32 [2, 640], P('section', 'tensor'), may hold values from -1.5 to 1.5
- ln3_gain: float32 [2, 640], P('section', 'tensor'), may hold values from 0.5 to 1.5
- ln3_bias: float32 [2, 640], P('section', 'tensor'), may hold values from -1.5 to 1.5
- w_out: bfloat16 [2, 640, 1280], P('section', 'tensor'), may hold values from -0.25 to 0.25
- b_out: float32 [2, 1280], P('section', 'tensor'), may hold values from -1.5 to 1.5
- cotangent: bfloat16 [16, 1280, 1024], P('batch', 'tensor'), may hold values from -6 to 6
Outputs:
- block_outputs: bfloat16 [2, 16, 1280, 1024], P('section', 'batch', 'tensor')
- input_grads: bfloat16 [2, 16, 1280, 1024], P('section', 'batch', 'tensor')
- grad_ln1_gain: float32 [2, 1280], P('section', 'tensor')
- grad_ln1_bias: float32 [2, 1280], P('section', 'tensor')
- grad_w_in: float32 [2, 640, 1280], P('section', 'tensor')
- grad_b_in: float32 [2, 640], P('section', 'tensor')
- grad_ln2_gain: float32 [2, 640], P('section', 'tensor')
- grad_ln2_bias: float32 [2, 640], P('section', 'tensor')
- grad_w_mix: float32 [2, 5, 640, 640], P('section', None, 'tensor')
- grad_b_mix: float32 [2, 640], P('section', 'tensor')
- grad_ln3_gain: float32 [2, 640], P('section', 'tensor')
- grad_ln3_bias: float32 [2, 640], P('section', 'tensor')
- grad_w_out: float32 [2, 640, 1280], P('section', 'tensor')
- grad_b_out: float32 [2, 1280], P('section', 'tensor')
The draws below stay inside these ranges and needn't reach their ends.
Inputs may be any that keep to these rules, and one draw needn't show every extreme that they name: `lengths`: some protein has length 1024 in every draw.
All inputs are finite; a program needn't handle non-finite values.
Results may differ from the reference program's by a relative error of at most 0.024.
Values may be sent and summed in bfloat16 or wider, within the bound.
No kernel may reach another device: no remote copies, remote signals or barrier semaphores. Data moves between devices by JAX's collectives and lax.ppermute only.
A program may use at most 256 MiB of HBM per device.

```python
import jax
import jax.numpy as jnp
from jax import lax

D = 1280
HID = 640
KERNEL_WIDTH = 5
L = 1024
SHORTEST = 30
NEAR_DILATION = 2
BROAD_DILATION = 128
PER_MICRO = 1
PROTEINS = 16


def draw_lengths(key, part):
    key = jax.random.fold_in(key, 11)
    first_key, second_key = jax.random.split(key)
    base = jax.random.randint(first_key, (PROTEINS,), SHORTEST, L + 1)
    chosen = jax.random.randint(second_key, (), 0, PROTEINS)
    return jnp.where(jnp.arange(PROTEINS) == chosen, L, base).astype(jnp.int32)


def shard_levels(rng, shape, cuts, smallest, largest):
    loudness = 1.0
    for dim, shards_of in cuts:
        heights = jax.random.uniform(jax.random.fold_in(jax.random.fold_in(rng, 6), dim), (shards_of,), jnp.float32, smallest / len(cuts), largest / len(cuts))
        loudness = loudness * jnp.repeat(jnp.exp(heights), shape[dim] // shards_of).reshape((-1,) + (1,) * (len(shape) - 1 - dim))
    return loudness


def centred(own_key, shape, scale, limit, shards=(), held_as=jnp.bfloat16):
    loudness = shard_levels(own_key, shape, shards, -0.22, 0.18) if shards else 1.0
    drawn = jax.random.normal(own_key, shape, jnp.float32) * scale * loudness
    return jnp.minimum(jnp.maximum(drawn, -limit), limit).astype(held_as)


def setup_inputs(seed: int = 0) -> dict:
    streams_of = jax.random.split(jax.random.key(seed), 16)
    return {
        "tokens": centred(streams_of[0], (PROTEINS, D, L), 1.0, 6.0, ((0, 4), (1, 4))),
        "lengths": draw_lengths(jax.random.fold_in(streams_of[15], 71), 0),
        "ln1_gain": jnp.clip(1.0 + 0.1 * jax.random.normal(streams_of[2], (2, D), jnp.float32), 0.5, 1.5),
        "ln1_bias": centred(streams_of[3], (2, D), 0.3, 1.5, ((0, 2), (1, 4)), jnp.float32),
        "w_in": centred(streams_of[4], (2, HID, D), D ** -0.5, 0.15625, ((0, 2), (1, 4))),
        "b_in": centred(streams_of[5], (2, HID), 0.3, 1.5, ((0, 2), (1, 4)), jnp.float32),
        "ln2_gain": jnp.clip(1.0 + 0.1 * jax.random.normal(streams_of[6], (2, HID), jnp.float32), 0.5, 1.5),
        "ln2_bias": centred(streams_of[7], (2, HID), 0.3, 1.5, ((0, 2), (1, 4)), jnp.float32),
        "w_mix": centred(streams_of[8], (2, KERNEL_WIDTH, HID, HID), (KERNEL_WIDTH * HID) ** -0.5, 0.109375, ((0, 2), (2, 4))),
        "b_mix": centred(streams_of[9], (2, HID), 0.3, 1.5, ((0, 2), (1, 4)), jnp.float32),
        "ln3_gain": jnp.clip(1.0 + 0.1 * jax.random.normal(streams_of[10], (2, HID), jnp.float32), 0.5, 1.5),
        "ln3_bias": centred(streams_of[11], (2, HID), 0.3, 1.5, ((0, 2), (1, 4)), jnp.float32),
        "w_out": centred(streams_of[12], (2, HID, D), HID ** -0.5, 0.25, ((0, 2), (1, 4))),
        "b_out": centred(streams_of[13], (2, D), 0.3, 1.5, ((0, 2), (1, 4)), jnp.float32),
        "cotangent": centred(streams_of[14], (PROTEINS, D, L), 1.0, 6.0, ((0, 4), (1, 4))),
    }


@jax.custom_vjp
def lower_bound(v):
    return lax.optimization_barrier(v.astype(jnp.bfloat16)).astype(jnp.float32)

@jax.custom_vjp
def lower_bound_reverse(v):
    return v

def low_keep(v):
    return (lower_bound(v), None)

def low_pass(kept, grad):
    return (grad,)

def back_keep(v):
    return (v, None)

def back_low(kept, grad):
    return (lower_bound(grad),)
lower_bound.defvjp(low_keep, low_pass)
lower_bound_reverse.defvjp(back_keep, back_low)
HIGH = lax.Precision.HIGHEST

def layer_norm(value, gain, bias):
    mean = lax.optimization_barrier(jnp.mean(value, -1, keepdims=True))
    spread = lax.optimization_barrier(jnp.mean(jnp.square(value - mean), -1, keepdims=True))
    return (value - mean) * lax.rsqrt(spread + 1e-05) * gain + bias

def dilated(inputs, weight, dilation_rate):
    taps = weight.shape[0]
    halo_margin = taps // 2 * dilation_rate
    padded = jnp.pad(inputs, ((0, 0), (halo_margin, halo_margin), (0, 0)))
    length = inputs.shape[1]
    total = jnp.zeros(inputs.shape[:2] + (weight.shape[2],), jnp.float32)
    for k in range(taps):
        piece = padded[:, k * dilation_rate:k * dilation_rate + length]
        total = total + jnp.einsum('nlc,co->nlo', piece, weight[k], precision=HIGH)
    return total

def block_params(x, token_mask, params, dilation_rate):
    gain1, bias1, w_in, b_in, gain2, bias2, w_mix, b_mix, gain3, bias3, w_out, b_out = params
    act1 = lower_bound(jax.nn.gelu(layer_norm(x, gain1, bias1)))
    hid1 = lower_bound_reverse(jnp.einsum('nld,dh->nlh', act1, w_in, precision=HIGH) + b_in)
    act2 = lower_bound(jax.nn.gelu(layer_norm(hid1, gain2, bias2)) * token_mask)
    hid3 = lower_bound_reverse(dilated(act2, w_mix, dilation_rate) + b_mix)
    act3 = lower_bound(jax.nn.gelu(layer_norm(hid3, gain3, bias3)))
    branch = jnp.einsum('nlh,hd->nld', act3, w_out, precision=HIGH) + b_out
    return x + branch * token_mask

def reference(tokens, lengths, ln1_gain, ln1_bias, w_in, b_in, ln2_gain, ln2_bias, w_mix, b_mix, ln3_gain, ln3_bias, w_out, b_out, cotangent):
    w_in_rows = jnp.transpose(w_in.astype(jnp.float32), (0, 2, 1))
    w_mix_rows = jnp.transpose(w_mix.astype(jnp.float32), (0, 1, 3, 2))
    params = tuple((a.astype(jnp.float32) for a in (ln1_gain, ln1_bias, w_in_rows, b_in, ln2_gain, ln2_bias, w_mix_rows, b_mix, ln3_gain, ln3_bias, w_out, b_out)))
    first = tuple((p[0] for p in params))
    second = tuple((p[1] for p in params))
    groups = PROTEINS // PER_MICRO
    inputs = jnp.transpose(tokens.astype(jnp.float32), (0, 2, 1)).reshape(groups, PER_MICRO, L, D)
    cots = jnp.transpose(cotangent.astype(jnp.float32), (0, 2, 1)).reshape(groups, PER_MICRO, L, D)
    lens = lengths.reshape(groups, PER_MICRO)

    def step(totals, item):
        x, cot, length_row = item
        token_mask = (jnp.arange(L, dtype=jnp.int32)[None, :] < length_row[:, None]).astype(jnp.float32)[:, :, None]

        def forward(first_params, second_params, block_input, small_perturbation):
            first_output = lower_bound(block_params(block_input, token_mask, first_params, NEAR_DILATION))
            second_output = block_params(lower_bound_reverse(first_output + small_perturbation), token_mask, second_params, BROAD_DILATION)
            return (first_output, second_output)
        zeros = jnp.zeros_like(x)
        (first_output, second_output), pull = jax.vjp(forward, first, second, x, zeros)
        g_first, g_second, g_x, g_mid = pull((zeros, cot))
        totals = jax.tree.map(lambda a, b: a + b, totals, (g_first, g_second))
        return (totals, (first_output.astype(jnp.bfloat16), second_output.astype(jnp.bfloat16), g_x.astype(jnp.bfloat16), g_mid.astype(jnp.bfloat16)))
    start = (tuple((jnp.zeros_like(p) for p in first)), tuple((jnp.zeros_like(p) for p in second)))
    totals, (ys_first, ys_second, gs_x, gs_mid) = lax.scan(step, start, (inputs, cots, lens))

    def flip(value):
        return jnp.transpose(value.reshape(PROTEINS, L, D), (0, 2, 1))
    block_outputs = jnp.stack([flip(ys_first), flip(ys_second)])
    input_grads = jnp.stack([flip(gs_x), flip(gs_mid)])
    grads = [jnp.stack([a, b]) for a, b in zip(totals[0], totals[1])]
    grads[2] = jnp.transpose(grads[2], (0, 2, 1))
    grads[6] = jnp.transpose(grads[6], (0, 1, 3, 2))
    return (block_outputs, input_grads) + tuple(grads)
```

```python
import functools

import jax
import jax.numpy as jnp
from jax import lax
from jax.experimental import pallas as pl
from jax.experimental.pallas import tpu as pltpu
from jax.sharding import PartitionSpec as P

D = 1280
HID = 640
KERNEL_WIDTH = 5
NEAR_DILATION = 2
BROAD_DILATION = 128
MICRO = 4


EPS = 1e-05
BF = jnp.bfloat16
F32 = jnp.float32
C0 = 0.7978845608028654
C1 = C0 * 0.044715
ROWS = 16
CHUNK = 256
TAPS = KERNEL_WIDTH * HID
WIDE = D + TAPS + D
EXTRA = 256
VMEM_LIMIT = 58 * 2**20
G1, B1, BI, G2, B2, BM, G3, B3, BO = 0, 1280, 2560, 3200, 3840, 4480, 5120, 5760, 6400
PARAM_ROWS = 7680
V_G1, V_B1, V_BO, V_BI, V_G2, V_B2, V_BM, V_G3, V_B3 = range(9)


def spread(column, length):
    return jnp.concatenate([column] * (length // 128), axis=1)


def block_rows(i):
    return pl.ds(pl.multiple_of(i * ROWS, ROWS), ROWS)


def columns(j, width=CHUNK):
    return pl.ds(pl.multiple_of(j * width, width), width)


def loop(count, body, init=None, unroll=1):
    if init is None:
        lax.fori_loop(0, count, lambda i, c: (body(i), c)[1], 0, unroll=unroll)
        return None
    return lax.fori_loop(0, count, body, init, unroll=unroll)


def fold(value):
    total = value[:8]
    for i in range(1, value.shape[0] // 8):
        total = total + value[8 * i : 8 * i + 8]
    return total


def lane_fold(value):
    total = value[:, :128]
    for i in range(1, value.shape[1] // 128):
        total = total + value[:, 128 * i : 128 * i + 128]
    return total


def channel_stats(load, count, length):
    base = load(0)[0:1]

    def body(i, carry):
        value = load(i) - base
        return carry[0] + fold(value), carry[1] + fold(value * value)

    zero = jnp.zeros((8, length), F32)
    total, square = loop(count, body, (zero, zero), unroll=2)
    width = float(count * ROWS)
    mean = jnp.sum(total, 0, keepdims=True) / width
    var = jnp.sum(square, 0, keepdims=True) / width - mean * mean
    scale = lax.rsqrt(jnp.maximum(var, 0.0) + EPS)
    return mean + base, scale


def half_gate(n, n2):
    return 0.5 * jnp.tanh(n * (C1 * n2 + C0)) + 0.5


def gelu(n):
    return n * half_gate(n, n * n)


def gelu_and_slope(n):
    n2 = n * n
    half = half_gate(n, n2)
    act = n * half
    slope = half + act * (1.0 - half) * (6.0 * C1 * n2 + 2.0 * C0)
    return act, slope


def shifted(value, by):
    if by == 0:
        return value
    length = value.shape[1]
    moved = pltpu.roll(value, (-by) % length, 1)
    lane = lax.broadcasted_iota(jnp.int32, value.shape, 1)
    keep = lane < length - by if by > 0 else lane >= -by
    return jnp.where(keep, moved, 0.0)


def mask_row(length, valid):
    return (lax.broadcasted_iota(jnp.int32, (1, length), 1) < valid).astype(F32)


def nn(a, b):
    return jnp.dot(a, b, preferred_element_type=F32)


def nt(a, b):
    return lax.dot_general(a, b, (((1,), (1,)), ((), ())), preferred_element_type=F32)


def tn(a, b):
    return lax.dot_general(a, b, (((0,), (0,)), ((), ())), preferred_element_type=F32)


def gather_pieces(refs, target, own, sems, first, onward):
    count = len(refs)
    per = target.shape[0] // count
    copies = []
    for s, ref in enumerate(refs):
        source = lax.rem(own + s if onward else own + count - s, count)
        copies.append(
            pltpu.make_async_copy(
                ref, target.at[pl.ds(pl.multiple_of(source * per, ROWS), per)], sems.at[first + s]
            )
        )
    return copies


def scatter_pieces(source, refs, own, sems, first):
    count = len(refs)
    per = source.shape[0] // count
    copies = []
    for s, ref in enumerate(refs):
        owner = lax.rem(own + s, count)
        copies.append(
            pltpu.make_async_copy(
                source.at[pl.ds(pl.multiple_of(owner * per, ROWS), per)], ref, sems.at[first + s]
            )
        )
    return copies


def start(copies):
    for copy in copies:
        copy.start()


def wait(copies):
    for copy in copies:
        copy.wait()


def forward_kernel(role, dilation, parts, *refs):
    ctl = refs[0]
    x_in = refs[1 : 1 + parts]
    w_hbm, prm_hbm = refs[1 + parts : 3 + parts]
    y_out = refs[3 + parts : 3 + 2 * parts]
    h1_out, h3_out, st_out = refs[3 + 2 * parts : 6 + 2 * parts]
    x, a1, h, st, stack, a3, w1, w2, w3, prm, y, sems = refs[6 + 2 * parts :]
    length = x.shape[1]
    chunks = length // CHUNK

    @pl.when(ctl[0] == role)
    def _():
        own = ctl[1]
        mask = mask_row(length, ctl[2])
        loads = gather_pieces(x_in, x, own, sems, 0, role == 1)
        base = parts
        first = pltpu.make_async_copy(w_hbm.at[:, pl.ds(0, D)], w1, sems.at[base])
        taps = pltpu.make_async_copy(w_hbm.at[:, pl.ds(D, TAPS)], w2, sems.at[base + 1])
        last = pltpu.make_async_copy(w_hbm.at[:, pl.ds(D + TAPS, D)], w3, sems.at[base + 2])
        params = pltpu.make_async_copy(prm_hbm, prm, sems.at[base + 3])
        start(loads)
        params.start()
        first.start()
        taps.start()
        last.start()
        wait(loads)
        params.wait()

        def par(offset, i):
            return spread(prm[pl.ds(pl.multiple_of(offset + i * ROWS, ROWS), ROWS)], length)

        def normed_of(load, i, mean, scale, gain, bias):
            return (load(i) - mean) * scale * par(gain, i) + par(bias, i)

        def load_x(i):
            return x[block_rows(i)].astype(F32)

        def load_h1(i):
            return h[0, block_rows(i)]

        def load_h3(i):
            return h[1, block_rows(i)]

        mean1, scale1 = channel_stats(load_x, D // ROWS, length)

        def act1(i):
            a1[block_rows(i)] = gelu(normed_of(load_x, i, mean1, scale1, G1, B1)).astype(BF)

        loop(D // ROWS, act1)
        first.wait()
        bias_in = spread(prm[pl.ds(BI, HID)], CHUNK)

        def hidden1(j):
            h[0, :, columns(j)] = nn(w1[...], a1[:, columns(j)]) + bias_in

        loop(chunks, hidden1)
        save1 = pltpu.make_async_copy(h.at[0], h1_out, sems.at[base + 4])
        save1.start()
        mean2, scale2 = channel_stats(load_h1, HID // ROWS, length)

        def act2(i):
            value = gelu(normed_of(load_h1, i, mean2, scale2, G2, B2)) * mask
            for k in range(KERNEL_WIDTH):
                rows = pl.ds(pl.multiple_of(k * HID + i * ROWS, ROWS), ROWS)
                stack[rows] = shifted(value, (k - KERNEL_WIDTH // 2) * dilation).astype(BF)

        loop(HID // ROWS, act2)
        taps.wait()
        bias_mix = spread(prm[pl.ds(BM, HID)], CHUNK)

        def hidden3(j):
            h[1, :, columns(j)] = nn(w2[...], stack[:, columns(j)]) + bias_mix

        loop(chunks, hidden3)
        save3 = pltpu.make_async_copy(h.at[1], h3_out, sems.at[base + 5])
        save3.start()
        mean3, scale3 = channel_stats(load_h3, HID // ROWS, length)
        for row, value in enumerate((mean1, scale1, mean2, scale2, mean3, scale3)):
            st[row : row + 1] = value
        save_st = pltpu.make_async_copy(st, st_out, sems.at[base + 6])
        save_st.start()

        def act3(i):
            a3[block_rows(i)] = gelu(normed_of(load_h3, i, mean3, scale3, G3, B3)).astype(BF)

        loop(HID // ROWS, act3)
        last.wait()
        bias_out = spread(prm[pl.ds(BO, D)], CHUNK)

        def result(j):
            keep = (
                lax.broadcasted_iota(jnp.int32, (1, CHUNK), 1) + j * CHUNK < ctl[2]
            ).astype(F32)
            branch = tn(w3[...], a3[:, columns(j)]) + bias_out
            y[:, columns(j)] = (x[:, columns(j)].astype(F32) + branch * keep).astype(BF)

        loop(chunks, result)
        stores = scatter_pieces(y, y_out, own, sems, base + 7)
        start(stores)
        wait(stores)
        save1.wait()
        save3.wait()
        save_st.wait()


def backward_kernel(role, dilation, parts, *refs):
    ctl = refs[0]
    x_in = refs[1 : 1 + parts]
    gy_in = refs[1 + parts : 1 + 2 * parts]
    h1_hbm, h3_hbm, st_hbm, w_hbm, wt_hbm, w1t_hbm, prm_hbm = refs[1 + 2 * parts : 8 + 2 * parts]
    gx_out = refs[8 + 2 * parts : 8 + 3 * parts]
    keep_out = refs[8 + 3 * parts : 14 + 3 * parts]
    vec_out = refs[14 + 3 * parts]
    rest = refs[15 + 3 * parts :]
    x, gy, dz, h, grad, grad1, stack, a3, a2, a1, dh1, st, vec, w1, w2, w3, prm, sems = rest
    length = x.shape[1]
    chunks = length // CHUNK

    @pl.when(ctl[0] == role)
    def _():
        own = ctl[1]
        mask = mask_row(length, ctl[2])
        base = 3 * parts
        loads_gy = gather_pieces(gy_in, gy, own, sems, 0, role == 0)
        loads_x = gather_pieces(x_in, x, own, sems, parts, role == 1)

        def copy_in(src, dst, index):
            return pltpu.make_async_copy(src, dst, sems.at[base + index])

        params = copy_in(prm_hbm, prm, 0)
        in_st = copy_in(st_hbm, st, 1)
        in_h3 = copy_in(h3_hbm, h.at[1], 2)
        in_h1 = copy_in(h1_hbm, h.at[0], 3)
        last = copy_in(w_hbm.at[:, pl.ds(D + TAPS, D)], w3, 4)
        taps = copy_in(wt_hbm, w2, 5)
        first = copy_in(w1t_hbm, w1, 6)
        start(loads_gy)
        start((last, in_st, params, in_h3, taps, in_h1))
        start(loads_x)
        first.start()
        vec[...] = jnp.zeros_like(vec)
        lane16 = lax.broadcasted_iota(jnp.int32, (ROWS, 128), 1)

        def add_vec(i, entries):
            total = vec[block_rows(i)]
            for index, value in entries:
                total = total + jnp.where(
                    lane16 == index, jnp.sum(lane_fold(value), 1, keepdims=True), 0.0
                )
            vec[block_rows(i)] = total

        def par(offset, i):
            return spread(prm[pl.ds(pl.multiple_of(offset + i * ROWS, ROWS), ROWS)], length)

        wait(loads_gy)

        def mask_gy(i):
            value = gy[block_rows(i)].astype(F32) * mask
            dz[block_rows(i)] = value.astype(BF)
            add_vec(i, ((V_BO, value),))

        loop(D // ROWS, mask_gy)
        save_dz = copy_in(dz, keep_out[5], 7)
        save_dz.start()
        last.wait()

        def grad_a3(j):
            grad[:, columns(j)] = nn(w3[...], dz[:, columns(j)])

        loop(chunks, grad_a3)
        params.wait()
        in_st.wait()
        in_h3.wait()

        def norm_back(load, count, offset, gain, bias, source, act_ref, act_mask, v_gain, v_bias, emit):
            mean, scale = st[offset : offset + 1], st[offset + 1 : offset + 2]

            def gather(i, carry):
                normed = (load(i) - mean) * scale
                gains = par(gain, i)
                act, slope = gelu_and_slope(normed * gains + par(bias, i))
                if act_mask is not None:
                    act = act * act_mask
                act_ref[block_rows(i)] = act.astype(BF)
                rows = block_rows(i)
                dn = slope * source[rows]
                if act_mask is not None:
                    dn = dn * act_mask
                lifted = dn * normed
                add_vec(i, ((v_gain, lifted), (v_bias, dn)))
                scaled = dn * gains
                source[rows] = scaled
                return carry[0] + fold(scaled), carry[1] + fold(lifted * gains)

            zero = jnp.zeros((8, length), F32)
            total, product = loop(count, gather, (zero, zero))
            width = float(count * ROWS)
            shift = jnp.sum(total, 0, keepdims=True) / width
            tilt = jnp.sum(product, 0, keepdims=True) / width

            def finish(i):
                normed = (load(i) - mean) * scale
                emit(i, scale * (source[block_rows(i)] - shift - normed * tilt))

            loop(count, finish)

        def emit3(i, value):
            low = value.astype(BF).astype(F32)
            add_vec(i, ((V_BM, low),))
            for k in range(KERNEL_WIDTH):
                rows = pl.ds(pl.multiple_of(k * HID + i * ROWS, ROWS), ROWS)
                stack[rows] = shifted(low, (KERNEL_WIDTH // 2 - k) * dilation).astype(BF)

        norm_back(
            lambda i: h[1, block_rows(i)], HID // ROWS, 4, G3, B3, grad, a3, None, V_G3, V_B3, emit3
        )
        save_a3 = copy_in(a3, keep_out[0], 8)
        save_stack = copy_in(stack, keep_out[4], 9)
        save_a3.start()
        save_stack.start()
        taps.wait()

        def grad_a2(j):
            grad[:, columns(j)] = nn(w2[...], stack[:, columns(j)])

        loop(chunks, grad_a2)
        in_h1.wait()

        def emit2(i, value):
            low = value.astype(BF)
            add_vec(i, ((V_BI, low.astype(F32)),))
            dh1[block_rows(i)] = low

        norm_back(
            lambda i: h[0, block_rows(i)], HID // ROWS, 2, G2, B2, grad, a2, mask, V_G2, V_B2, emit2
        )
        save_a2 = copy_in(a2, keep_out[1], 10)
        save_dh1 = copy_in(dh1, keep_out[3], 11)
        save_a2.start()
        save_dh1.start()
        first.wait()

        def grad_a1(j):
            grad1[:, columns(j)] = nn(w1[...], dh1[:, columns(j)])

        loop(chunks, grad_a1)
        wait(loads_x)

        def emit1(i, value):
            rows = block_rows(i)
            gy[rows] = (gy[rows].astype(F32) + value).astype(BF)

        norm_back(
            lambda i: x[block_rows(i)].astype(F32),
            D // ROWS,
            0,
            G1,
            B1,
            grad1,
            a1,
            None,
            V_G1,
            V_B1,
            emit1,
        )
        stores = scatter_pieces(gy, gx_out, own, sems, 2 * parts)
        start(stores)
        save_a1 = copy_in(a1, keep_out[2], 12)
        save_vec = copy_in(vec, vec_out, 13)
        save_a1.start()
        save_vec.start()
        wait(stores)
        wait((save_dz, save_a3, save_stack, save_a2, save_dh1, save_a1, save_vec))


def weight_kernel(role, parts, *refs):
    ctl, a3_hbm, a2_hbm, a1_hbm, dh1_hbm, stack_hbm, dz_hbm, vec_hbm = refs[:8]
    if role == 0:
        refs = refs[1:]
    out = refs[8]
    a3, a2, a1, dh1, stack, dz, vec, total, sems = refs[9:]

    @pl.when(ctl[0] == role)
    def _():
        copies = [
            pltpu.make_async_copy(src, dst, sems.at[i])
            for i, (src, dst) in enumerate(
                (
                    (a3_hbm, a3),
                    (dz_hbm, dz),
                    (vec_hbm, vec),
                    (a2_hbm, a2),
                    (stack_hbm, stack),
                    (dh1_hbm, dh1),
                    (a1_hbm, a1),
                )
            )
        ]
        start(copies)
        wait(copies[:3])
        per = HID // parts
        for z in range(parts):
            rows = slice(per * z, per * z + per)
            near, hidden = vec[2 * per * z : 2 * per * z + per], vec[per * z : per * z + per]
            lane = lax.broadcasted_iota(jnp.int32, near.shape, 1)
            total[rows, WIDE : WIDE + 128] = jnp.where(lane < V_BI, near, hidden).astype(BF)
            total[rows, WIDE + 128 :] = vec[2 * per * z + per : 2 * per * (z + 1)].astype(BF)

        def last(j):
            at = pl.ds(pl.multiple_of(D + TAPS + j * CHUNK, 128), CHUNK)
            total[:, at] = nt(a3[...], dz[columns(j)]).astype(BF)

        loop(D // CHUNK, last)
        wait(copies[3:5])

        def taps(k):
            rows = pl.ds(pl.multiple_of(k * HID, HID), HID)
            at = pl.ds(pl.multiple_of(D + k * HID, 128), HID)
            total[:, at] = nt(stack[rows], a2[...]).astype(BF)

        loop(KERNEL_WIDTH, taps)
        wait(copies[5:])

        def first(j):
            total[:, columns(j)] = nt(dh1[...], a1[columns(j)]).astype(BF)

        loop(D // CHUNK, first)
        done = pltpu.make_async_copy(total, out, sems.at[7])
        done.start()
        done.wait()


def turn_kernel(w_hbm, w1t_out, wt_out, w1, w2, t1, t2, sems):
    in1 = pltpu.make_async_copy(w_hbm.at[:, pl.ds(0, D)], w1, sems.at[0])
    in2 = pltpu.make_async_copy(w_hbm.at[:, pl.ds(D, TAPS)], w2, sems.at[1])
    in1.start()
    in2.start()
    in1.wait()

    def first(j):
        t1[columns(j, 128)] = w1[:, columns(j, 128)].T

    loop(D // 128, first)
    out1 = pltpu.make_async_copy(t1, w1t_out, sems.at[2])
    out1.start()
    in2.wait()

    def taps(j):
        k = j // (HID // 128)
        c = j - k * (HID // 128)
        at = pl.ds(pl.multiple_of(k * HID, 128), HID)
        t2[columns(c, 128), at] = w2[:, columns(j, 128)].T

    loop(TAPS // 128, taps)
    out2 = pltpu.make_async_copy(t2, wt_out, sems.at[3])
    out2.start()
    out1.wait()
    out2.wait()


ANY = pl.BlockSpec(memory_space=pl.ANY)
SMEM = pl.BlockSpec(memory_space=pltpu.SMEM)


def shape(*dims, dtype=BF):
    return jax.ShapeDtypeStruct(dims, dtype)


def cost(flops, moved):
    return pl.CostEstimate(flops=int(flops), bytes_accessed=int(moved), transcendentals=0)


def call(kernel, operands, outs, scratch, name, flops, aliases=None):
    return pl.pallas_call(
        kernel,
        out_shape=outs,
        in_specs=[SMEM if a.ndim == 1 else ANY for a in operands],
        out_specs=[ANY] * len(outs),
        scratch_shapes=scratch,
        input_output_aliases=aliases or {},
        compiler_params=pltpu.CompilerParams(vmem_limit_bytes=VMEM_LIMIT),
        cost_estimate=cost(flops, 30e6),
        name=name,
    )(*operands)


def run_forward(role, dilation, ctl, pieces, weights, params, length):
    parts = len(pieces)
    scratch = [
        pltpu.VMEM((D, length), BF),
        pltpu.VMEM((D, length), BF),
        pltpu.VMEM((2, HID, length), F32),
        pltpu.VMEM((8, length), F32),
        pltpu.VMEM((TAPS, length), BF),
        pltpu.VMEM((HID, length), BF),
        pltpu.VMEM((HID, D), BF),
        pltpu.VMEM((HID, TAPS), BF),
        pltpu.VMEM((HID, D), BF),
        pltpu.VMEM((PARAM_ROWS, 128), F32),
        pltpu.VMEM((D, length), BF),
        pltpu.SemaphoreType.DMA((2 * parts + 7,)),
    ]
    outs = [shape(D // parts, length)] * parts + [
        shape(HID, length, dtype=F32),
        shape(HID, length, dtype=F32),
        shape(8, length, dtype=F32),
    ]
    result = call(
        functools.partial(forward_kernel, role, dilation, parts),
        [ctl, *pieces, weights, params],
        outs,
        scratch,
        f"forward{role}",
        2 * HID * WIDE * length,
    )
    return result[:parts], result[parts:]


def run_backward(role, dilation, ctl, x_pieces, gy_pieces, saved, weights, turned, params, length):
    parts = len(x_pieces)
    scratch = [
        pltpu.VMEM((D, length), BF),
        pltpu.VMEM((D, length), BF),
        pltpu.VMEM((D, length), BF),
        pltpu.VMEM((2, HID, length), F32),
        pltpu.VMEM((HID, length), F32),
        pltpu.VMEM((D, length), F32),
        pltpu.VMEM((TAPS, length), BF),
        pltpu.VMEM((HID, length), BF),
        pltpu.VMEM((HID, length), BF),
        pltpu.VMEM((D, length), BF),
        pltpu.VMEM((HID, length), BF),
        pltpu.VMEM((8, length), F32),
        pltpu.VMEM((D, 128), F32),
        pltpu.VMEM((D, HID), BF),
        pltpu.VMEM((HID, TAPS), BF),
        pltpu.VMEM((HID, D), BF),
        pltpu.VMEM((PARAM_ROWS, 128), F32),
        pltpu.SemaphoreType.DMA((3 * parts + 14,)),
    ]
    outs = [shape(D // parts, length)] * parts + [
        shape(HID, length),
        shape(HID, length),
        shape(D, length),
        shape(HID, length),
        shape(TAPS, length),
        shape(D, length),
        shape(D, 128, dtype=F32),
    ]
    result = call(
        functools.partial(backward_kernel, role, dilation, parts),
        [ctl, *x_pieces, *gy_pieces, *saved, weights, turned[1], turned[0], params],
        outs,
        scratch,
        f"backward{role}",
        2 * HID * WIDE * length,
    )
    return result[:parts], result[parts:]


def run_weights(role, parts, ctl, kept, before, length):
    scratch = [
        pltpu.VMEM((HID, length), BF),
        pltpu.VMEM((HID, length), BF),
        pltpu.VMEM((D, length), BF),
        pltpu.VMEM((HID, length), BF),
        pltpu.VMEM((TAPS, length), BF),
        pltpu.VMEM((D, length), BF),
        pltpu.VMEM((D, 128), F32),
        pltpu.VMEM((HID, WIDE + EXTRA), BF),
        pltpu.SemaphoreType.DMA((8,)),
    ]
    operands = [ctl, *kept] + ([] if before is None else [before])
    return call(
        functools.partial(weight_kernel, role, parts),
        operands,
        [shape(HID, WIDE + EXTRA)],
        scratch,
        f"weights{role}",
        2 * HID * WIDE * length,
        None if before is None else {8: 0},
    )[0]


def run_turn(weights):
    return call(
        turn_kernel,
        [weights],
        [shape(D, HID), shape(HID, TAPS)],
        [
            pltpu.VMEM((HID, D), BF),
            pltpu.VMEM((HID, TAPS), BF),
            pltpu.VMEM((D, HID), BF),
            pltpu.VMEM((HID, TAPS), BF),
            pltpu.SemaphoreType.DMA((4,)),
        ],
        "turn_weights",
        0,
    )


def from_behind(x, axis, by):
    length = lax.axis_size(axis)
    pairs = [(i, i + by) for i in range(length) if 0 <= i + by < length]
    return lax.ppermute(x, axis, pairs)


def as_sent(x):

    def short(part):
        return part.astype(jnp.bfloat16) if part.dtype == jnp.float32 else part

    return jax.tree.map(short, x)


def norm_forward(value, gain, bias, width):
    sums = lax.psum(
        (jnp.sum(value, 1, keepdims=True), jnp.sum(value * value, 1, keepdims=True)), "tensor"
    )
    mean = sums[0] / width
    scale = lax.rsqrt(sums[1] / width - mean * mean + EPS)
    normed = (value - mean) * scale
    return (normed * gain + bias, normed, scale)


def norm_backward(grad_out, normed, scale, gain, width):
    scaled = grad_out * gain
    sums = lax.psum(
        (jnp.sum(scaled, 1, keepdims=True), jnp.sum(scaled * normed, 1, keepdims=True)), "tensor"
    )
    return scale * (scaled - sums[0] / width - normed * sums[1] / width)


def gelu_slope(value, grad):
    return jax.vjp(jax.nn.gelu, value)[1](grad)[0]


def row_total(value):
    return jnp.sum(value, axis=(0, 2))


def tap_stack(inputs, dilation_rate):
    halo_margin = KERNEL_WIDTH // 2 * BROAD_DILATION
    length = inputs.shape[2]
    padded = jnp.pad(inputs, ((0, 0), (0, 0), (halo_margin, halo_margin)))
    pieces = [
        lax.dynamic_slice_in_dim(
            padded, halo_margin + (k - KERNEL_WIDTH // 2) * dilation_rate, length, 2
        )
        for k in range(KERNEL_WIDTH)
    ]
    return jnp.stack(pieces, 1)


def tap_unstack(spread, dilation_rate):
    halo_margin = KERNEL_WIDTH // 2 * BROAD_DILATION
    length = spread.shape[3]
    padded = jnp.pad(spread, ((0, 0), (0, 0), (0, 0), (halo_margin, halo_margin)))
    total = jnp.zeros((spread.shape[0], spread.shape[2], length), jnp.float32)
    for k in range(KERNEL_WIDTH):
        total = total + lax.dynamic_slice_in_dim(
            padded[:, k], halo_margin - (k - KERNEL_WIDTH // 2) * dilation_rate, length, 2
        )
    return total


def block_forward(inputs, token_mask, weights, dilation_rate):
    gain1, bias1, w_first, c_first, gain2, bias2, w_taps, c_mix, gain3, bias3, w_last, c_last = (
        weights
    )
    value = inputs.astype(jnp.float32)
    pre1, normed1, scale1 = norm_forward(value, gain1, bias1, D)
    act1 = jax.nn.gelu(pre1).astype(jnp.bfloat16)
    act1_full = lax.all_gather(act1, "tensor", axis=1, tiled=True)
    hidden1 = (
        jnp.einsum("pdl,hd->phl", act1_full, w_first, preferred_element_type=jnp.float32) + c_first
    )
    pre2, normed2, scale2 = norm_forward(hidden1, gain2, bias2, HID)
    act2 = (jax.nn.gelu(pre2) * token_mask).astype(jnp.bfloat16)
    act2_full = lax.all_gather(act2, "tensor", axis=1, tiled=True)
    hidden3 = (
        jnp.einsum(
            "pkcl,koc->pol",
            tap_stack(act2_full, dilation_rate),
            w_taps,
            preferred_element_type=jnp.float32,
        )
        + c_mix
    )
    pre3, normed3, scale3 = norm_forward(hidden3, gain3, bias3, HID)
    act3 = jax.nn.gelu(pre3).astype(jnp.bfloat16)
    partial_out = jnp.einsum("phl,hd->pdl", act3, w_last, preferred_element_type=jnp.float32)
    branch = (
        lax.psum_scatter(
            partial_out.astype(jnp.bfloat16), "tensor", scatter_dimension=1, tiled=True
        ).astype(jnp.float32)
        + c_last
    )
    kept = (
        pre1,
        normed1,
        scale1,
        act1_full,
        pre2,
        normed2,
        scale2,
        act2_full,
        pre3,
        normed3,
        scale3,
        act3,
    )
    return (value + branch * token_mask, kept)


def block_backward(grad_y, token_mask, weights, dilation_rate, kept):
    gain1, bias1, w_first, c_first, gain2, bias2, w_taps, c_mix, gain3, bias3, w_last, c_last = (
        weights
    )
    (
        pre1,
        normed1,
        scale1,
        act1_full,
        pre2,
        normed2,
        scale2,
        act2_full,
        pre3,
        normed3,
        scale3,
        act3,
    ) = kept
    grad_z = grad_y * token_mask.astype(jnp.bfloat16)
    grad_z_full = lax.all_gather(grad_z, "tensor", axis=1, tiled=True)
    grad_c_last = row_total(grad_z.astype(jnp.float32))
    grad_w_last = jnp.einsum("phl,pdl->hd", act3, grad_z_full, preferred_element_type=jnp.float32)
    grad_act3 = jnp.einsum("pdl,hd->phl", grad_z_full, w_last, preferred_element_type=jnp.float32)
    grad_pre3 = gelu_slope(pre3, grad_act3)
    grad_gain3 = row_total(grad_pre3 * normed3)
    grad_bias3 = row_total(grad_pre3)
    grad_h3 = norm_backward(grad_pre3, normed3, scale3, gain3, HID).astype(jnp.bfloat16)
    grad_c_mix = row_total(grad_h3.astype(jnp.float32))
    grad_w_taps = jnp.einsum(
        "pkcl,pol->koc",
        tap_stack(act2_full, dilation_rate),
        grad_h3,
        preferred_element_type=jnp.float32,
    )
    spread = jnp.einsum("pol,koc->pkcl", grad_h3, w_taps, preferred_element_type=jnp.float32)
    grad_act2 = (
        lax.psum_scatter(
            tap_unstack(spread, dilation_rate).astype(jnp.bfloat16),
            "tensor",
            scatter_dimension=1,
            tiled=True,
        ).astype(jnp.float32)
        * token_mask
    )
    grad_pre2 = gelu_slope(pre2, grad_act2)
    grad_gain2 = row_total(grad_pre2 * normed2)
    grad_bias2 = row_total(grad_pre2)
    grad_h1 = norm_backward(grad_pre2, normed2, scale2, gain2, HID).astype(jnp.bfloat16)
    grad_c_first = row_total(grad_h1.astype(jnp.float32))
    grad_w_first = jnp.einsum("pdl,phl->hd", act1_full, grad_h1, preferred_element_type=jnp.float32)
    partial_in = jnp.einsum("phl,hd->pdl", grad_h1, w_first, preferred_element_type=jnp.float32)
    grad_act1 = lax.psum_scatter(
        partial_in.astype(jnp.bfloat16), "tensor", scatter_dimension=1, tiled=True
    ).astype(jnp.float32)
    grad_pre1 = gelu_slope(pre1, grad_act1)
    grad_gain1 = row_total(grad_pre1 * normed1)
    grad_bias1 = row_total(grad_pre1)
    grad_x = grad_y.astype(jnp.float32) + norm_backward(grad_pre1, normed1, scale1, gain1, D)
    terms = (
        grad_gain1,
        grad_bias1,
        grad_w_first,
        grad_c_first,
        grad_gain2,
        grad_bias2,
        grad_w_taps,
        grad_c_mix,
        grad_gain3,
        grad_bias3,
        grad_w_last,
        grad_c_last,
    )
    return (grad_x, terms)


def split_local(
    tokens,
    lengths,
    ln1_gain,
    ln1_bias,
    w_in,
    b_in,
    ln2_gain,
    ln2_bias,
    w_mix,
    b_mix,
    ln3_gain,
    ln3_bias,
    w_out,
    b_out,
    cotangent,
):
    relay_segment = lax.axis_index("section")
    weights = (
        ln1_gain[0][:, None],
        ln1_bias[0][:, None],
        w_in[0],
        b_in[0][:, None],
        ln2_gain[0][:, None],
        ln2_bias[0][:, None],
        w_mix[0],
        b_mix[0][:, None],
        ln3_gain[0][:, None],
        ln3_bias[0][:, None],
        w_out[0],
        b_out[0][:, None],
    )
    dilation_rate = jnp.where(relay_segment == 0, NEAR_DILATION, BROAD_DILATION).astype(jnp.int32)
    per = tokens.shape[0] // MICRO
    length = tokens.shape[2]
    masks = (jnp.arange(length, dtype=jnp.int32)[None, :] < lengths[:, None]).astype(jnp.float32)[
        :, None, :
    ]

    def rows_of(array, index):
        return lax.slice_in_dim(array, index * per, (index + 1) * per, axis=0)

    received = jnp.zeros_like(rows_of(tokens, 0))
    forward_ticks = []
    saved = []
    for tick in range(MICRO + 1):
        own = min(tick, MICRO - 1)
        token_mask = jnp.where(
            relay_segment == 0, rows_of(masks, own), rows_of(masks, max(tick - 1, 0))
        )
        inputs = jnp.where(relay_segment == 0, rows_of(tokens, own), received)
        result, kept = block_forward(inputs, token_mask, weights, dilation_rate)
        result = result.astype(jnp.bfloat16)
        forward_ticks.append(result)
        saved.append((token_mask, inputs))
        received = from_behind(result, "section", 1)
    incoming = jnp.zeros_like(received)
    backward_ticks = []
    totals = None
    for tick in range(MICRO + 1):
        token_mask, stash = saved[MICRO - tick]
        kept = block_forward(stash, token_mask, weights, dilation_rate)[1]
        start = jnp.where(
            relay_segment == 1, rows_of(cotangent, max(MICRO - 1 - tick, 0)), incoming
        )
        grad_x, terms = block_backward(start, token_mask, weights, dilation_rate, kept)
        valid = jnp.where(relay_segment == 0, float(tick >= 1), float(tick < MICRO)).astype(
            jnp.float32
        )
        terms = tuple((valid * term for term in terms))
        totals = terms if totals is None else tuple((a + b for a, b in zip(totals, terms)))
        sent = grad_x.astype(jnp.bfloat16)
        backward_ticks.append(sent)
        incoming = from_behind(sent, "section", -1)
    forward_rows = [
        jnp.where(relay_segment == 0, forward_ticks[j], forward_ticks[j + 1]) for j in range(MICRO)
    ]
    backward_rows = [
        jnp.where(relay_segment == 0, backward_ticks[MICRO - j], backward_ticks[MICRO - 1 - j])
        for j in range(MICRO)
    ]
    block_outputs = jnp.concatenate(forward_rows, 0)[None]
    input_grads = jnp.concatenate(backward_rows, 0)[None]
    summed = jax.tree.map(lambda part: part.astype(jnp.float32), lax.psum(as_sent(totals), "batch"))
    return (block_outputs, input_grads) + tuple((value[None] for value in summed))


def hop(pieces, source, target):
    return [lax.ppermute(p, "section", [(source, target)]) for p in pieces]


def exchange(pieces, role, parts):
    got = []
    for s in range(1, parts):
        pairs = [
            (role * parts + i, role * parts + (i + s) % parts) for i in range(parts)
        ]
        got.append(lax.ppermute(pieces[s], ("section", "tensor"), pairs))
    return [pieces[0]] + got


def pick(a, section):
    return jnp.where(section == 0, a[0], a[1])


def by_protein(pieces, own):
    count = len(pieces)
    stack = jnp.stack(pieces)
    order = lax.rem(own + count - jnp.arange(count, dtype=jnp.int32), count)
    return jnp.take(stack, order, axis=0)


def parallel_local(
    tokens,
    lengths,
    ln1_gain,
    ln1_bias,
    w_in,
    b_in,
    ln2_gain,
    ln2_bias,
    w_mix,
    b_mix,
    ln3_gain,
    ln3_bias,
    w_out,
    b_out,
    cotangent,
):
    section = lax.axis_index("section")
    own = lax.axis_index("tensor")
    parts = lax.axis_size("tensor")
    batch = lax.axis_size("batch")
    length = tokens.shape[2]
    per = HID // parts
    ctl = jnp.stack([section, own, jnp.take(lengths, own)]).astype(jnp.int32)

    shard = jnp.concatenate(
        [w_in[0], jnp.swapaxes(w_mix[0], 0, 1).reshape(per, TAPS), w_out[0]], axis=1
    )
    share = per // batch
    mine = lax.dynamic_slice_in_dim(shard, lax.axis_index("batch") * share, share, 0)
    weights = lax.all_gather(mine, ("tensor", "batch"), axis=0, tiled=True)
    vectors = jnp.concatenate(
        [a[0] for a in (ln1_gain, ln1_bias, b_in, ln2_gain, ln2_bias, b_mix, ln3_gain, ln3_bias, b_out)]
    )
    table = lax.all_gather(vectors, "tensor", axis=0, tiled=False)
    rows, at = [], 0
    for width in (2, 2, 1, 1, 1, 1, 1, 1, 2):
        rows.append(table[:, at * per : (at + width) * per].reshape(-1))
        at += width
    params = jnp.broadcast_to(jnp.concatenate(rows)[:, None], (PARAM_ROWS, 128))

    source = jnp.where(section == 0, tokens, cotangent)
    sent = [lax.dynamic_index_in_dim(source, lax.rem(own + s, parts), 0, False) for s in range(parts)]
    given = [sent[0]]
    for s in range(1, parts):
        given.append(
            lax.ppermute(sent[s], "tensor", [(i, (i + s) % parts) for i in range(parts)])
        )

    y1, saved0 = run_forward(0, NEAR_DILATION, ctl, given, weights, params, length)
    turned = run_turn(weights)
    middle = hop(y1, 0, 1)
    y2, saved1 = run_forward(1, BROAD_DILATION, ctl, middle, weights, params, length)
    g1, kept1 = run_backward(
        1, BROAD_DILATION, ctl, middle, given, saved1, weights, turned, params, length
    )
    back = hop(g1, 1, 0)
    total = run_weights(1, parts, ctl, kept1, None, length)
    g0, kept0 = run_backward(
        0, NEAR_DILATION, ctl, given, back, saved0, weights, turned, params, length
    )
    total = run_weights(0, parts, ctl, kept0, total, length)

    out1 = by_protein(exchange(y1, 0, parts), own)
    out2 = by_protein(exchange(y2, 1, parts), own)
    in1 = by_protein(exchange(g1, 1, parts), own)
    in0 = by_protein(exchange(g0, 0, parts), own)
    block_outputs = jnp.where(section == 0, out1, out2)[None]
    input_grads = jnp.where(section == 0, in0, in1)[None]

    mine = lax.psum_scatter(total, ("tensor", "batch"), scatter_dimension=0, tiled=True)
    full = lax.all_gather(mine, "batch", axis=0, tiled=True).astype(F32)
    grad_in = full[:, :D]
    grad_mix = jnp.swapaxes(full[:, D : D + TAPS].reshape(per, KERNEL_WIDTH, HID), 0, 1)
    grad_out = full[:, D + TAPS : WIDE]
    near, far = full[:, WIDE : WIDE + 128], full[:, WIDE + 128 :]

    def wide(index):
        return jnp.concatenate([near[:, index], far[:, index]])

    def narrow(index):
        return near[:, index]

    grads = (
        wide(V_G1),
        wide(V_B1),
        grad_in,
        narrow(V_BI),
        narrow(V_G2),
        narrow(V_B2),
        grad_mix,
        narrow(V_BM),
        narrow(V_G3),
        narrow(V_B3),
        grad_out,
        wide(V_BO),
    )
    return (block_outputs, input_grads) + tuple(value[None] for value in grads)


def solution(mesh):
    placed = (
        P("batch", "tensor", None),
        P("batch"),
        P("section", "tensor"),
        P("section", "tensor"),
        P("section", "tensor", None),
        P("section", "tensor"),
        P("section", "tensor"),
        P("section", "tensor"),
        P("section", None, "tensor", None),
        P("section", "tensor"),
        P("section", "tensor"),
        P("section", "tensor"),
        P("section", "tensor", None),
        P("section", "tensor"),
        P("batch", "tensor", None),
    )
    def local(tokens, *rest):
        if tokens.shape[0] == mesh.shape["tensor"]:
            return parallel_local(tokens, *rest)
        return split_local(tokens, *rest)

    return jax.shard_map(
        local,
        mesh=mesh,
        in_specs=placed,
        out_specs=(
            P("section", "batch", "tensor", None),
            P("section", "batch", "tensor", None),
            P("section", "tensor"),
            P("section", "tensor"),
            P("section", "tensor", None),
            P("section", "tensor"),
            P("section", "tensor"),
            P("section", "tensor"),
            P("section", None, "tensor", None),
            P("section", "tensor"),
            P("section", "tensor"),
            P("section", "tensor"),
            P("section", "tensor", None),
            P("section", "tensor"),
        ),
        check_vma=False,
    )
```
